32 devices in a mesh: expert: 8 (over y, x, core), tensor: 4 (over z).
Axes of the slice: x: 2, y: 2, z: 4, core: 2. Of those that a mesh axis runs over, the one named last changes fastest.
Arguments:
- tokens: bfloat16 [8192, 1024], P(('expert', 'tensor')), may hold values from -6 to 6
- segment_ids: int32 [8192], P('expert'), may hold values from 0 to 2, as said below
- expert_ids: int32 [8192, 8], P(('expert', 'tensor')), may hold values from 0 to 31, as said below
- slot_ids: int32 [8192, 8], P(('expert', 'tensor')), may hold values from -1 to 63, as said below
- norm1_gain: float32 [1024], replicated, may hold values from 0.5 to 1.5
- w_query: bfloat16 [1024, 1024], P(None, 'tensor'), may hold values from -2 to 2
- w_key: bfloat16 [1024, 512], P(None, 'tensor'), may hold values from -2 to 2
- w_value: bfloat16 [1024, 512], P(None, 'tensor'), may hold values from -0.1875 to 0.1875
- w_out: bfloat16 [1024, 1024], P('tensor'), may hold values from -6 to 6
- norm2_gain: float32 [1024], replicated, may hold values from 0.5 to 1.5
- w_router: bfloat16 [1024, 32], replicated, may hold values from -0.25 to 0.25
- w_gate: bfloat16 [32, 1024, 512], P('expert', None, 'tensor'), may hold values from -0.1875 to 0.1875
- w_up: bfloat16 [32, 1024, 512], P('expert', None, 'tensor'), may hold values from -0.1875 to 0.1875
- w_down: bfloat16 [32, 512, 1024], P('expert', 'tensor'), may hold values from -6 to 6
- cotangent: bfloat16 [8192, 1024], P(('expert', 'tensor')), may hold values from -6 to 6
Outputs:
- mixed: bfloat16 [8192, 1024], P(('expert', 'tensor'))
- grad_input: float32 [8192, 1024], P(('expert', 'tensor'))
- grad_norm1: float32 [1024], replicated
- grad_query: float32 [1024, 1024], P(None, 'tensor')
- grad_key: float32 [1024, 512], P(None, 'tensor')
- grad_value: float32 [1024, 512], P(None, 'tensor')
- grad_out_proj: float32 [1024, 1024], P('tensor')
- grad_norm2: float32 [1024], replicated
- grad_router: float32 [1024, 32], replicated
- grad_gate: float32 [32, 1024, 512], P('expert', None, 'tensor')
- grad_up: float32 [32, 1024, 512], P('expert', None, 'tensor')
- grad_down: float32 [32, 512, 1024], P('expert', 'tensor')
The draws below stay inside these ranges and needn't reach their ends.
Inputs may be any that keep to these rules, and one draw needn't show every extreme that they name: `segment_ids`: each sequence of 1024 tokens holds documents 0, 1 and 2 in order; document 0 ends within the first 256 positions of its sequence and document 2 begins within the last 256. `expert_ids`: each row names 8 different experts. `slot_ids`: in each aligned block of 256 rows, a choice's slot is the number of earlier choices of the same expert in that block, counted in order of rows and then of choices, and -1 where that number is 64 or more; some expert fills all 64 slots of every block.
All inputs are finite; a program needn't handle non-finite values.
Results may differ from the reference program's by a relative error of at most 0.018.
The reference program's roundings to bfloat16 on the way count: a program that leaves them out, or rounds other values in their place, can miss the bound.
Values may be sent and summed in bfloat16 or wider, within the bound.
A program may use at most 192 MiB of HBM per device.

```python
import jax
import jax.numpy as jnp
from jax import lax

D = 1024
HEADS = 16
KV = 8
HDIM = 64
FF = 512
EXPERTS = 32
TOPK = 8
SEQ = 1024
ROWS_DEV = 256
CAP = 64
TOKENS = 8192
N_EXPERT = 8
N_TENSOR = 4


def routing(key):
    blocks = TOKENS // ROWS_DEV
    key_hot, key_perm, key_offset, key_lead = jax.random.split(key, 4)
    hottest = jax.random.randint(key_hot, (), 0, EXPERTS)
    orders = jax.vmap(lambda one_key: jax.random.permutation(one_key, EXPERTS))(jax.random.split(key_perm, blocks))
    leading = orders[:, :1]
    orders = jnp.where(orders == hottest, leading, orders)
    orders = orders.at[:, 0].set(hottest)
    offsets = jax.random.randint(key_offset, (blocks, ROWS_DEV), 0, EXPERTS)
    leaders = (jax.random.randint(key_lead, (blocks, CAP), 0, TOPK) + EXPERTS - TOPK + 1) % EXPERTS
    offsets = offsets.at[:, :CAP].set(leaders)
    places = (offsets[:, :, None] + jnp.arange(TOPK)[None, None, :]) % EXPERTS
    chosen = jax.vmap(lambda order_row, place_rows: order_row[place_rows])(orders, places)
    flat_ids = chosen.reshape(blocks, ROWS_DEV * TOPK)
    hits = (flat_ids[:, :, None] == jnp.arange(EXPERTS)[None, None, :]).astype(jnp.int32)
    ranked = jnp.sum(jnp.cumsum(hits, axis=1) * hits, axis=2) - 1
    slotted = jnp.where(ranked < CAP, ranked, -1)
    return (chosen.reshape(TOKENS, TOPK).astype(jnp.int32), slotted.reshape(TOKENS, TOPK).astype(jnp.int32))


def draw_expert_ids(key, part):
    return routing(key)[0]


def draw_slot_ids(key, part):
    return routing(key)[1]


def draw_segment_ids(key, part):
    key = jax.random.fold_in(key, 7)
    key_first, key_last = jax.random.split(key, 2)
    sequences = TOKENS // SEQ
    first_end = jax.random.randint(key_first, (sequences, 1), 1, ROWS_DEV)
    last_start = jax.random.randint(key_last, (sequences, 1), SEQ - ROWS_DEV + 1, SEQ)
    position = jnp.arange(SEQ)[None, :]
    numbers = (position >= first_end).astype(jnp.int32) + (position >= last_start).astype(jnp.int32)
    return numbers.reshape(TOKENS).astype(jnp.int32)


def level_of(stream_key, shape, cuts, least, high):
    level, own = 1.0, jax.random.fold_in(stream_key, 6)
    for dim, blocks in cuts:
        draws = jnp.exp(jax.random.uniform(jax.random.fold_in(own, dim), (blocks,), jnp.float32, least / len(cuts), high / len(cuts)))
        level = level * jnp.repeat(draws, shape[dim] // blocks).reshape([-1 if axis == dim else 1 for axis in range(len(shape))])
    return level


def bell_draw(own_key, shape, spread, most, shards=(), held_as=jnp.bfloat16):
    result = spread * jax.random.normal(own_key, shape, jnp.float32)
    if shards:
        result = result * level_of(own_key, shape, shards, -0.22, 0.18)
    return jnp.clip(result, -most, most).astype(held_as)


def setup_inputs(seed: int = 0) -> dict:
    streams_of = jax.random.split(jax.random.key(seed), 16)
    tokens = bell_draw(streams_of[0], (TOKENS, D), 1.0, 6.0, ((0, 32),))
    segment_ids = draw_segment_ids(jax.random.fold_in(streams_of[15], 71), 0)
    expert_ids = draw_expert_ids(jax.random.fold_in(streams_of[15], 71), 0)
    slot_ids = draw_slot_ids(jax.random.fold_in(streams_of[15], 71), 0)
    norm1_gain = jnp.clip(1.0 + 0.1 * jax.random.normal(streams_of[4], (D,), jnp.float32), 0.5, 1.5)
    w_query = bell_draw(streams_of[5], (D, HEADS * HDIM), (4 * D ** -0.5), 2.0, ((1, 4),))
    w_key = bell_draw(streams_of[6], (D, KV * HDIM), (4 * D ** -0.5), 2.0, ((1, 4),))
    w_value = bell_draw(streams_of[7], (D, KV * HDIM), D ** -0.5, 0.1875, ((1, 4),))
    w_out = bell_draw(streams_of[8], (HEADS * HDIM, D), (48 * (HEADS * HDIM) ** -0.5), 6.0, ((0, 4),))
    norm2_gain = jnp.clip(1.0 + 0.1 * jax.random.normal(streams_of[9], (D,), jnp.float32), 0.5, 1.5)
    w_router = bell_draw(streams_of[10], (D, EXPERTS), (0.5 * D ** -0.5), 0.25)
    w_gate = bell_draw(streams_of[11], (EXPERTS, D, FF), D ** -0.5, 0.1875, ((0, 8), (2, 4)))
    w_up = bell_draw(streams_of[12], (EXPERTS, D, FF), D ** -0.5, 0.1875, ((0, 8), (2, 4)))
    w_down = bell_draw(streams_of[13], (EXPERTS, FF, D), (12 * FF ** -0.5), 6.0, ((0, 8), (1, 4)))
    cotangent = bell_draw(streams_of[14], (TOKENS, D), 1.0, 6.0, ((0, 32),))
    return {"tokens": tokens, "segment_ids": segment_ids, "expert_ids": expert_ids, "slot_ids": slot_ids, "norm1_gain": norm1_gain, "w_query": w_query, "w_key": w_key, "w_value": w_value, "w_out": w_out, "norm2_gain": norm2_gain, "w_router": w_router, "w_gate": w_gate, "w_up": w_up, "w_down": w_down, "cotangent": cotangent}


EPSILON = 1e-06
RESIDUAL = 0.22
MASKED = -1e+30
ATTENTION_MULTIPLIER = 0.015625
HIGHEST_MODE = lax.Precision.HIGHEST

@jax.custom_vjp
def low(v):
    return lax.optimization_barrier(v.astype(jnp.bfloat16)).astype(jnp.float32)

@jax.custom_vjp
def low_back(v):
    return v

def low_keep(v):
    return (low(v), None)

def low_pass(kept, grad):
    return (grad,)

def back_keep(v):
    return (v, None)

def back_low(kept, grad):
    return (low(grad),)
low.defvjp(low_keep, low_pass)
low_back.defvjp(back_keep, back_low)

def normed(rows, gain):
    return rows * lax.rsqrt(lax.optimization_barrier(jnp.mean(rows * rows, axis=-1, keepdims=True)) + EPSILON) * gain

def rope_tables(positions, width):
    half_width = width // 2
    frequency = 10000.0 ** (-(jnp.arange(half_width, dtype=jnp.float32) * 2.0) / width)
    angles = positions[:, None] * frequency[None, :]
    cos_table = jnp.concatenate([jnp.cos(angles), jnp.cos(angles)], axis=-1)
    sine_table = jnp.concatenate([jnp.sin(angles), jnp.sin(angles)], axis=-1)
    return (cos_table[:, None, :], sine_table[:, None, :])

def rotate(head_vals, cos_table, sine_table):
    half_width = head_vals.shape[-1] // 2
    turned = jnp.concatenate([-head_vals[..., half_width:], head_vals[..., :half_width]], axis=-1)
    return head_vals * cos_table + turned * sine_table

def matmul(left, right):
    return jnp.dot(left, right, preferred_element_type=jnp.float32, precision=HIGHEST_MODE)

def attend_sequence(pieces):
    queries, keys_in, values_in, segments = pieces
    length = queries.shape[0]
    group_size = HEADS // KV
    grouped = queries.reshape(length, KV, group_size, HDIM)
    raw_scores = jnp.einsum('qkgd,skd->kgqs', grouped, keys_in, precision=HIGHEST_MODE) * ATTENTION_MULTIPLIER
    raw_scores = low_back(raw_scores)
    index = jnp.arange(length)
    allowed = (index[:, None] >= index[None, :]) & (segments[:, None] == segments[None, :])
    raw_scores = jnp.where(allowed[None, None], raw_scores, MASKED)
    probability = low(jax.nn.softmax(raw_scores, axis=-1))
    mixed_heads = jnp.einsum('kgqs,skd->qkgd', probability, values_in, precision=HIGHEST_MODE)
    return mixed_heads.reshape(length, HEADS * HDIM)

def expert_apply(pieces):
    rows_in, gate_w, up_w, down_w = pieces
    gate_act = low_back(matmul(rows_in, gate_w))
    up_act = low_back(matmul(rows_in, up_w))
    hidden = low(jax.nn.silu(gate_act) * up_act)
    return low_back(low(matmul(hidden, down_w)))

def reference(tokens, segment_ids, expert_ids, slot_ids, norm1_gain, w_query, w_key, w_value, w_out, norm2_gain, w_router, w_gate, w_up, w_down, cotangent):
    floats = tuple((item.astype(jnp.float32) for item in (tokens, norm1_gain, w_query, w_key, w_value, w_out, norm2_gain, w_router, w_gate, w_up, w_down)))
    positions = (jnp.arange(TOKENS, dtype=jnp.int32) % SEQ).astype(jnp.float32)
    cos_table, sine_table = rope_tables(positions, HDIM)
    per_expert = N_EXPERT * N_TENSOR * CAP
    block_of = jnp.arange(TOKENS, dtype=jnp.int32) // ROWS_DEV
    kept = slot_ids >= 0
    target = jnp.where(kept, expert_ids * per_expert + block_of[:, None] * CAP + slot_ids, EXPERTS * per_expert).astype(jnp.int32)
    selector = (expert_ids[:, :, None] == jnp.arange(EXPERTS, dtype=jnp.int32)[None, None, :]).astype(jnp.float32)
    sequences = TOKENS // SEQ

    def forward(inputs_f, gain_one, query_w, key_w, value_w, out_w, gain_two, router_w, gate_w, up_w, down_w):
        normed_one = low(normed(inputs_f, gain_one))
        query_raw = low_back(matmul(normed_one, query_w)).reshape(TOKENS, HEADS, HDIM)
        queries = low(rotate(query_raw, cos_table, sine_table))
        key_raw = low_back(matmul(normed_one, key_w)).reshape(TOKENS, KV, HDIM)
        keys_all = low(rotate(key_raw, cos_table, sine_table))
        values_all = low(low_back(matmul(normed_one, value_w))).reshape(TOKENS, KV, HDIM)
        head_out = lax.map(jax.checkpoint(attend_sequence), (queries.reshape(sequences, SEQ, HEADS, HDIM), keys_all.reshape(sequences, SEQ, KV, HDIM), values_all.reshape(sequences, SEQ, KV, HDIM), segment_ids.reshape(sequences, SEQ)))
        head_out = low_back(low(head_out.reshape(TOKENS, HEADS * HDIM)))
        attn = low_back(matmul(head_out, out_w))
        residual = inputs_f + RESIDUAL * attn
        normed_two = low(normed(residual, gain_two))
        router_logits = low_back(matmul(normed_two, router_w))
        gate_weights = jax.nn.softmax(lax.optimization_barrier(jnp.sum(selector * router_logits[:, None, :], axis=-1)), axis=-1)
        slots_buffer = jnp.zeros((EXPERTS * per_expert, D), jnp.float32)
        for slot_pick in range(TOPK):
            slots_buffer = slots_buffer.at[target[:, slot_pick]].set(low_back(normed_two), mode='drop')
        expert_out = lax.map(jax.checkpoint(expert_apply), (slots_buffer.reshape(EXPERTS, per_expert, D), gate_w, up_w, down_w))
        expert_flat = expert_out.reshape(EXPERTS * per_expert, D)
        expert_mix = jnp.zeros_like(residual)
        for slot_pick in range(TOPK):
            picked = jnp.take(expert_flat, jnp.minimum(target[:, slot_pick], EXPERTS * per_expert - 1), axis=0)
            picked = jnp.where(kept[:, slot_pick, None], picked, 0.0)
            expert_mix = expert_mix + gate_weights[:, slot_pick, None] * picked
        return residual + RESIDUAL * expert_mix
    output, backward = jax.vjp(forward, *floats)
    grads = backward(cotangent.astype(jnp.float32))
    return (output.astype(jnp.bfloat16), grads[0], grads[1], grads[2], grads[3], grads[4], grads[5], grads[6], grads[7], grads[8], grads[9], grads[10])
```

```python
import jax
import jax.numpy as jnp
from jax import lax
from jax.experimental import pallas as pl
from jax.experimental.pallas import tpu as pltpu
from jax.sharding import PartitionSpec as P

HDIM = 64


EPSILON = 1e-06
RESIDUAL = 0.22
MASKED = -1e30
ATTENTION_MULTIPLIER = 0.015625


def normed(rows, gain):
    return rows * lax.rsqrt(jnp.mean(rows * rows, axis=-1, keepdims=True) + EPSILON) * gain


def rope_tables(positions, width):
    half_width = width // 2
    frequency = 10000.0 ** (-(jnp.arange(half_width, dtype=jnp.float32) * 2.0) / width)
    angles = positions[:, None] * frequency[None, :]
    cos_table = jnp.concatenate([jnp.cos(angles), jnp.cos(angles)], axis=-1)
    sine_table = jnp.concatenate([jnp.sin(angles), jnp.sin(angles)], axis=-1)
    return (cos_table[:, None, :], sine_table[:, None, :])


def rotate(head_vals, cos_table, sine_table):
    half_width = head_vals.shape[-1] // 2
    turned = jnp.concatenate([-head_vals[..., half_width:], head_vals[..., :half_width]], axis=-1)
    return head_vals * cos_table + turned * sine_table


def contract_rows(left, right):
    return lax.dot_general(
        left, right, (((0,), (0,)), ((), ())), preferred_element_type=jnp.float32
    )


def contract_cols(left, right):
    return lax.dot_general(
        left, right, (((1,), (1,)), ((), ())), preferred_element_type=jnp.float32
    )


def per_device_slots(
    tokens,
    segment_ids,
    expert_ids,
    slot_ids,
    norm1_gain,
    w_query,
    w_key,
    w_value,
    w_out,
    norm2_gain,
    w_router,
    w_gate,
    w_up,
    w_down,
    cotangent,
):
    rows_dev, model_width = tokens.shape
    top_count = expert_ids.shape[1]
    experts = w_router.shape[1]
    capacity = rows_dev * top_count // experts
    head_dim = HDIM
    key_heads = w_key.shape[1] // head_dim
    query_heads = w_query.shape[1] // head_dim
    group_size = query_heads // key_heads
    score_scale = ATTENTION_MULTIPLIER
    length = segment_ids.shape[0]
    block_rows = min(length, 512)
    blocks = length // block_rows
    inputs_f = tokens.astype(jnp.float32)
    normed_one_f, norm_one_back = jax.vjp(normed, inputs_f, norm1_gain)
    normed_one = normed_one_f.astype(jnp.bfloat16)
    whole_rows = lax.all_gather(normed_one, "tensor", axis=0, tiled=True)
    cos_table, sine_table = rope_tables(jnp.arange(length).astype(jnp.float32), head_dim)
    query_raw = jnp.dot(whole_rows, w_query, preferred_element_type=jnp.float32).reshape(
        length, query_heads, head_dim
    )
    key_raw = jnp.dot(whole_rows, w_key, preferred_element_type=jnp.float32).reshape(
        length, key_heads, head_dim
    )
    queries = (
        rotate(query_raw, cos_table, sine_table)
        .astype(jnp.bfloat16)
        .reshape(length, key_heads, group_size, head_dim)
    )
    keys_all = rotate(key_raw, cos_table, sine_table).astype(jnp.bfloat16)
    values_all = (
        jnp.dot(whole_rows, w_value, preferred_element_type=jnp.float32)
        .astype(jnp.bfloat16)
        .reshape(length, key_heads, head_dim)
    )
    key_index = jnp.arange(length)

    def scores(query_block, row_start):
        row_index = row_start + jnp.arange(block_rows)
        seg_rows = lax.dynamic_slice_in_dim(segment_ids, row_start, block_rows)
        allowed = (row_index[:, None] >= key_index[None, :]) & (
            seg_rows[:, None] == segment_ids[None, :]
        )
        raw_scores = (
            jnp.einsum("qkgd,skd->kgqs", query_block, keys_all, preferred_element_type=jnp.float32)
            * score_scale
        )
        return jnp.where(allowed[None, None], raw_scores, MASKED)

    query_blocks = queries.reshape(blocks, block_rows, key_heads, group_size, head_dim)
    row_starts = jnp.arange(blocks, dtype=jnp.int32) * block_rows

    def forward_block(block_items):
        query_block, row_start = block_items
        logits = scores(query_block, row_start)
        peak_score = jnp.max(logits, axis=-1, keepdims=True)
        weights = jnp.exp(logits - peak_score)
        row_total = jnp.sum(weights, axis=-1, keepdims=True)
        probability = (weights / row_total).astype(jnp.bfloat16)
        mixed_heads = jnp.einsum(
            "kgqs,skd->qkgd", probability, values_all, preferred_element_type=jnp.float32
        )
        return (mixed_heads.astype(jnp.bfloat16), (peak_score + jnp.log(row_total))[..., 0])

    head_out, log_totals = lax.map(forward_block, (query_blocks, row_starts))
    head_out = head_out.reshape(length, query_heads * head_dim)
    row_part = head_out
    attn = lax.psum_scatter(
        jnp.dot(row_part, w_out, preferred_element_type=jnp.float32),
        "tensor",
        scatter_dimension=0,
        tiled=True,
    )
    residual = inputs_f + RESIDUAL * attn
    normed_two_f, norm_two_back = jax.vjp(normed, residual, norm2_gain)
    normed_two = normed_two_f.astype(jnp.bfloat16)
    router_logits = jnp.dot(normed_two, w_router, preferred_element_type=jnp.float32)
    selector = (expert_ids[:, :, None] == jnp.arange(experts)[None, None, :]).astype(jnp.float32)

    def gating(logit_rows):
        return jax.nn.softmax(jnp.sum(selector * logit_rows[:, None, :], axis=-1), axis=-1)

    gate_weights, gating_back = jax.vjp(gating, router_logits)
    target = jnp.where(slot_ids >= 0, expert_ids * capacity + slot_ids, -1).reshape(
        rows_dev * top_count
    )
    onehot = (target[:, None] == jnp.arange(experts * capacity)[None, :]).astype(jnp.bfloat16)
    row_hot = jnp.sum(onehot.reshape(rows_dev, top_count, experts * capacity), axis=1)
    outgoing = (
        contract_rows(row_hot, normed_two)
        .astype(jnp.bfloat16)
        .reshape(experts, capacity, model_width)
    )
    arrived = lax.all_to_all(outgoing, "expert", split_axis=0, concat_axis=1, tiled=True)
    gate_w, up_w, down_w = (
        lax.all_gather(w_gate, "tensor", axis=2, tiled=True),
        lax.all_gather(w_up, "tensor", axis=2, tiled=True),
        lax.all_gather(w_down, "tensor", axis=1, tiled=True),
    )
    gate_act = jnp.einsum("erd,edf->erf", arrived, gate_w, preferred_element_type=jnp.float32)
    up_act = jnp.einsum("erd,edf->erf", arrived, up_w, preferred_element_type=jnp.float32)
    sigmoid_gate = jax.nn.sigmoid(gate_act)
    swish_act = gate_act * sigmoid_gate
    hidden = (swish_act * up_act).astype(jnp.bfloat16)
    expert_terms = jnp.einsum("erf,efd->erd", hidden, down_w, preferred_element_type=jnp.float32)
    returned = lax.all_to_all(
        expert_terms.astype(jnp.bfloat16), "expert", split_axis=1, concat_axis=0, tiled=True
    )
    picked = jnp.dot(
        onehot,
        returned.reshape(experts * capacity, model_width),
        preferred_element_type=jnp.float32,
    )
    picked = picked.reshape(rows_dev, top_count, model_width)
    expert_mix = jnp.sum(gate_weights[:, :, None] * picked, axis=1)
    mixed_out = (residual + RESIDUAL * expert_mix).astype(jnp.bfloat16)
    upstream = cotangent.astype(jnp.float32)
    grad_mix = RESIDUAL * upstream
    grad_gates = jnp.sum(picked * grad_mix[:, None, :], axis=-1)
    grad_picked = (
        (gate_weights[:, :, None] * grad_mix[:, None, :])
        .astype(jnp.bfloat16)
        .reshape(rows_dev * top_count, model_width)
    )
    grad_slots = (
        contract_rows(onehot, grad_picked)
        .astype(jnp.bfloat16)
        .reshape(experts, capacity, model_width)
    )
    grad_arrived = lax.all_to_all(grad_slots, "expert", split_axis=0, concat_axis=1, tiled=True)
    grad_down_w = jnp.einsum(
        "erf,erd->efd", hidden, grad_arrived, preferred_element_type=jnp.float32
    )
    grad_hidden = jnp.einsum(
        "erd,efd->erf", grad_arrived, down_w, preferred_element_type=jnp.float32
    )
    grad_gate_act = (
        grad_hidden * up_act * (sigmoid_gate * (1.0 + gate_act * (1.0 - sigmoid_gate)))
    ).astype(jnp.bfloat16)
    grad_up_act = (grad_hidden * swish_act).astype(jnp.bfloat16)
    grad_gate_w = jnp.einsum(
        "erd,erf->edf", arrived, grad_gate_act, preferred_element_type=jnp.float32
    )
    grad_up_w = jnp.einsum("erd,erf->edf", arrived, grad_up_act, preferred_element_type=jnp.float32)
    grad_rows_in = jnp.einsum(
        "erf,edf->erd", grad_gate_act, gate_w, preferred_element_type=jnp.float32
    )
    grad_rows_in = grad_rows_in + jnp.einsum(
        "erf,edf->erd", grad_up_act, up_w, preferred_element_type=jnp.float32
    )
    grad_gate_w, grad_up_w, grad_down_w = (
        lax.psum_scatter(
            grad_gate_w.astype(jnp.bfloat16), "tensor", scatter_dimension=2, tiled=True
        ).astype(jnp.float32),
        lax.psum_scatter(
            grad_up_w.astype(jnp.bfloat16), "tensor", scatter_dimension=2, tiled=True
        ).astype(jnp.float32),
        lax.psum_scatter(
            grad_down_w.astype(jnp.bfloat16), "tensor", scatter_dimension=1, tiled=True
        ).astype(jnp.float32),
    )
    grad_returned = lax.all_to_all(
        grad_rows_in.astype(jnp.bfloat16), "expert", split_axis=1, concat_axis=0, tiled=True
    )
    grad_normed_two = jnp.dot(
        onehot,
        grad_returned.reshape(experts * capacity, model_width),
        preferred_element_type=jnp.float32,
    )
    grad_normed_two = jnp.sum(grad_normed_two.reshape(rows_dev, top_count, model_width), axis=1)
    grad_logits = gating_back(grad_gates)[0].astype(jnp.bfloat16)
    grad_router = contract_rows(normed_two, grad_logits)
    grad_normed_two = grad_normed_two + contract_cols(grad_logits, w_router)
    grad_residual, grad_norm2 = norm_two_back(grad_normed_two)
    grad_residual = grad_residual + upstream
    grad_attn = (RESIDUAL * grad_residual).astype(jnp.bfloat16)
    grad_attn_all = lax.all_gather(grad_attn, "tensor", axis=0, tiled=True)
    grad_out_w = contract_rows(head_out, grad_attn_all)
    grad_heads = contract_cols(grad_attn_all, w_out).astype(jnp.bfloat16)
    grad_heads = grad_heads.reshape(blocks, block_rows, key_heads, group_size, head_dim)

    def backward_block(carried, block_items):
        grad_keys, grad_values = carried
        query_block, row_start, log_total, grad_block = block_items
        logits = scores(query_block, row_start)
        probability = jnp.exp(logits - log_total[..., None])
        grad_values = grad_values + jnp.einsum(
            "kgqs,qkgd->skd",
            probability.astype(jnp.bfloat16),
            grad_block,
            preferred_element_type=jnp.float32,
        )
        grad_probs = jnp.einsum(
            "qkgd,skd->kgqs", grad_block, values_all, preferred_element_type=jnp.float32
        )
        centre = jnp.sum(probability * grad_probs, axis=-1, keepdims=True)
        grad_scores = (probability * (grad_probs - centre)).astype(jnp.bfloat16)
        grad_query_block = (
            jnp.einsum("kgqs,skd->qkgd", grad_scores, keys_all, preferred_element_type=jnp.float32)
            * score_scale
        )
        grad_keys = (
            grad_keys
            + jnp.einsum(
                "kgqs,qkgd->skd", grad_scores, query_block, preferred_element_type=jnp.float32
            )
            * score_scale
        )
        return ((grad_keys, grad_values), grad_query_block)

    zero_keys = jnp.zeros((length, key_heads, head_dim), jnp.float32)
    (grad_keys, grad_values), grad_queries = lax.scan(
        backward_block, (zero_keys, zero_keys), (query_blocks, row_starts, log_totals, grad_heads)
    )
    grad_queries = grad_queries.reshape(length, query_heads, head_dim)
    _, rope_query_back = jax.vjp(
        lambda head_vals: rotate(head_vals, cos_table, sine_table), query_raw
    )
    _, rope_key_back = jax.vjp(lambda head_vals: rotate(head_vals, cos_table, sine_table), key_raw)
    grad_query_raw = (
        rope_query_back(grad_queries)[0]
        .astype(jnp.bfloat16)
        .reshape(length, query_heads * head_dim)
    )
    grad_key_raw = (
        rope_key_back(grad_keys)[0].astype(jnp.bfloat16).reshape(length, key_heads * head_dim)
    )
    grad_value_raw = grad_values.astype(jnp.bfloat16).reshape(length, key_heads * head_dim)
    grad_query_w = contract_rows(whole_rows, grad_query_raw)
    grad_key_w = contract_rows(whole_rows, grad_key_raw)
    grad_value_w = contract_rows(whole_rows, grad_value_raw)

    def row_part(values_in):
        return values_in

    summed = contract_cols(row_part(grad_query_raw), w_query)
    summed = summed + contract_cols(row_part(grad_key_raw), w_key)
    grad_normed_one = lax.psum_scatter(
        (summed + contract_cols(row_part(grad_value_raw), w_value)).astype(jnp.bfloat16),
        "tensor",
        scatter_dimension=0,
        tiled=True,
    ).astype(jnp.float32)
    grad_inputs, grad_norm1 = norm_one_back(grad_normed_one)
    grad_inputs = grad_inputs + grad_residual
    grad_query_w, grad_key_w, grad_value_w, grad_out_w = (
        lax.psum(grad_query_w.astype(jnp.bfloat16), "expert").astype(jnp.float32),
        lax.psum(grad_key_w.astype(jnp.bfloat16), "expert").astype(jnp.float32),
        lax.psum(grad_value_w.astype(jnp.bfloat16), "expert").astype(jnp.float32),
        lax.psum(grad_out_w.astype(jnp.bfloat16), "expert").astype(jnp.float32),
    )
    grad_norm1, grad_norm2, grad_router = lax.psum(
        (grad_norm1, grad_norm2, grad_router), ("expert", "tensor")
    )
    return (
        mixed_out,
        grad_inputs,
        grad_norm1,
        grad_query_w,
        grad_key_w,
        grad_value_w,
        grad_out_w,
        grad_norm2,
        grad_router,
        grad_gate_w,
        grad_up_w,
        grad_down_w,
    )


ROW_BLOCK = 256
VMEM_BYTES = 58 * 1024 * 1024
GATHER_LIMIT = 32 * 1024 * 1024


def dot_f32(left, right, left_dim, right_dim):
    return lax.dot_general(
        left,
        right,
        (((left_dim,), (right_dim,)), ((), ())),
        preferred_element_type=jnp.float32,
    )


def half_swap(values):
    width = values.shape[-1]
    half = HDIM // 2
    lane = lax.broadcasted_iota(jnp.int32, values.shape, 1)
    ahead = pltpu.roll(values, width - half, 1)
    behind = pltpu.roll(values, half, 1)
    first = (lane % HDIM) < half
    return jnp.where(first, ahead, behind), first


def rope_rows(values, cos_table, sine_table):
    swapped, first = half_swap(values)
    return values * cos_table + jnp.where(first, -swapped, swapped) * sine_table


def rope_rows_back(values, cos_table, sine_table):
    swapped, first = half_swap(values * sine_table)
    return values * cos_table + jnp.where(first, swapped, -swapped)


def block_mask(seg_col, seg_row, start, rows, keys):
    row_index = start + lax.broadcasted_iota(jnp.int32, (rows, keys), 0)
    key_index = lax.broadcasted_iota(jnp.int32, (rows, keys), 1)
    return (row_index >= key_index) & (seg_col[start : start + rows, :] == seg_row[:, :keys])


def attention_forward(
    q_raw, k_raw, values, cos_t, sin_t, seg_col, seg_row, heads_out, queries, keys_out
):
    length, q_width = q_raw.shape
    k_width = k_raw.shape[1]
    queries[...] = rope_rows(q_raw[...], cos_t[...], sin_t[...]).astype(jnp.bfloat16)
    keys_out[...] = rope_rows(k_raw[...], cos_t[:, :k_width], sin_t[:, :k_width]).astype(
        jnp.bfloat16
    )
    group = q_width // k_width
    rows = min(length, ROW_BLOCK)
    for start in range(0, length, rows):
        count = start + rows
        allowed = block_mask(seg_col, seg_row, start, rows, count)
        for head in range(q_width // HDIM):
            kv = head // group
            q_blk = queries[start:count, head * HDIM : (head + 1) * HDIM]
            k_blk = keys_out[:count, kv * HDIM : (kv + 1) * HDIM]
            v_blk = values[:count, kv * HDIM : (kv + 1) * HDIM]
            score = dot_f32(q_blk, k_blk, 1, 1) * ATTENTION_MULTIPLIER
            score = jnp.where(allowed, score, MASKED)
            weight = jnp.exp(score - jnp.max(score, axis=1, keepdims=True))
            prob = weight * (1.0 / jnp.sum(weight, axis=1, keepdims=True))
            out = dot_f32(prob.astype(jnp.bfloat16), v_blk, 1, 0)
            heads_out[start:count, head * HDIM : (head + 1) * HDIM] = out.astype(jnp.bfloat16)


def attention_backward(
    queries, keys, values, grad_heads, cos_t, sin_t, seg_col, seg_row, dq_out, dk_out, dv_out, dq, dk, dv
):
    length, q_width = queries.shape
    k_width = keys.shape[1]
    group = q_width // k_width
    rows = min(length, ROW_BLOCK)
    dk[...] = jnp.zeros_like(dk)
    dv[...] = jnp.zeros_like(dv)
    for start in range(0, length, rows):
        count = start + rows
        allowed = block_mask(seg_col, seg_row, start, rows, count)
        for head in range(q_width // HDIM):
            kv = head // group
            q_blk = queries[start:count, head * HDIM : (head + 1) * HDIM]
            g_blk = grad_heads[start:count, head * HDIM : (head + 1) * HDIM]
            k_blk = keys[:count, kv * HDIM : (kv + 1) * HDIM]
            v_blk = values[:count, kv * HDIM : (kv + 1) * HDIM]
            score = dot_f32(q_blk, k_blk, 1, 1) * ATTENTION_MULTIPLIER
            score = jnp.where(allowed, score, MASKED)
            weight = jnp.exp(score - jnp.max(score, axis=1, keepdims=True))
            prob = weight * (1.0 / jnp.sum(weight, axis=1, keepdims=True))
            grad_prob = dot_f32(g_blk, v_blk, 1, 1)
            centre = jnp.sum(prob * grad_prob, axis=1, keepdims=True)
            grad_score = (prob * (grad_prob - centre)).astype(jnp.bfloat16)
            dq[start:count, head * HDIM : (head + 1) * HDIM] = (
                dot_f32(grad_score, k_blk, 1, 0) * ATTENTION_MULTIPLIER
            )
            dk[:count, kv * HDIM : (kv + 1) * HDIM] += dot_f32(grad_score, q_blk, 0, 0)
            dv[:count, kv * HDIM : (kv + 1) * HDIM] += dot_f32(
                prob.astype(jnp.bfloat16), g_blk, 0, 0
            )
    dq_out[...] = rope_rows_back(dq[...], cos_t[...], sin_t[...]).astype(jnp.bfloat16)
    dk_out[...] = rope_rows_back(
        dk[...] * ATTENTION_MULTIPLIER, cos_t[:, :k_width], sin_t[:, :k_width]
    ).astype(jnp.bfloat16)
    dv_out[...] = dv[...].astype(jnp.bfloat16)


def expert_kernel(
    h2, dz, eid, loc, router, w_gu, w_dn, moe, dh2, grad_gu, grad_dn, grad_rt, xs, zs, ys, ds, hot, gate_s
):
    blocks, top, rows = eid.shape
    experts = router.shape[0]
    local_experts, _, double_hidden = w_gu.shape
    hidden_width = double_hidden // 2
    slots = hot.shape[1]
    cap = slots // local_experts

    @pl.when(pl.program_id(0) == 0)
    def _():
        grad_gu[...] = jnp.zeros_like(grad_gu)
        grad_dn[...] = jnp.zeros_like(grad_dn)
        grad_rt[...] = jnp.zeros_like(grad_rt)

    slot_index = lax.broadcasted_iota(jnp.int32, (slots, rows), 0)
    expert_index = lax.broadcasted_iota(jnp.int32, (experts, rows), 0)
    gates = []
    for b in range(blocks):
        h_blk = h2[b * rows : (b + 1) * rows, :]
        z_blk = dz[b * rows : (b + 1) * rows, :]
        logits = dot_f32(router[...], h_blk, 1, 1)
        chosen = [
            jnp.sum(
                jnp.where(expert_index == eid[b, k : k + 1, :], logits, 0.0), axis=0, keepdims=True
            )
            for k in range(top)
        ]
        peak = chosen[0]
        for k in range(1, top):
            peak = jnp.maximum(peak, chosen[k])
        powers = [jnp.exp(c - peak) for c in chosen]
        total = powers[0]
        for k in range(1, top):
            total = total + powers[k]
        gate = [p / total for p in powers]
        gates.append(gate)
        weighted = jnp.zeros((slots, rows), jnp.float32)
        chosen_hot = jnp.zeros((slots, rows), jnp.float32)
        for k in range(top):
            hit = slot_index == loc[b, k : k + 1, :]
            weighted = jnp.where(hit, gate[k], weighted)
            chosen_hot = jnp.where(hit, 1.0, chosen_hot)
        hot_b = chosen_hot.astype(jnp.bfloat16)
        hot[b] = hot_b
        gate_s[b] = jnp.sum(weighted, axis=1, keepdims=True)
        xs[b] = dot_f32(hot_b, h_blk, 1, 0).astype(jnp.bfloat16)
        zs[b] = dot_f32(hot_b, z_blk, 1, 0).astype(jnp.bfloat16)
    slot_grads = []
    for e in range(local_experts):
        span = slice(e * cap, (e + 1) * cap)
        x_e = xs[:, span, :].reshape(blocks * cap, -1)
        z_e = zs[:, span, :].reshape(blocks * cap, -1)
        gate_e = gate_s[:, span, :].reshape(blocks * cap, 1)
        both = dot_f32(x_e, w_gu[e], 1, 0)
        g_act, u_act = both[:, :hidden_width], both[:, hidden_width:]
        sig = 1.0 / (1.0 + jnp.exp(-g_act))
        swish = g_act * sig
        hid_f = swish * u_act
        hid = hid_f.astype(jnp.bfloat16)
        out = dot_f32(hid, w_dn[e], 1, 0)
        ys[:, span, :] = (gate_e * out).astype(jnp.bfloat16).reshape(blocks, cap, -1)
        grad_raw = dot_f32(z_e, w_dn[e], 1, 1) * RESIDUAL
        slot_grads.append(
            jnp.sum(hid.astype(jnp.float32) * grad_raw, axis=1, keepdims=True).reshape(
                blocks, cap, 1
            )
        )
        grad_hid = gate_e * grad_raw
        dg = grad_hid * u_act * (sig * (1.0 + g_act * (1.0 - sig)))
        du = grad_hid * swish
        dgu = jnp.concatenate([dg, du], axis=1).astype(jnp.bfloat16)
        scaled = (hid.astype(jnp.float32) * (gate_e * RESIDUAL)).astype(jnp.bfloat16)
        grad_dn[e] += dot_f32(scaled, z_e, 0, 0)
        grad_gu[e] += dot_f32(x_e, dgu, 0, 0)
        ds[:, span, :] = dot_f32(dgu, w_gu[e], 1, 1).astype(jnp.bfloat16).reshape(blocks, cap, -1)
    for b in range(blocks):
        h_blk = h2[b * rows : (b + 1) * rows, :]
        hot_b = hot[b]
        moe[b * rows : (b + 1) * rows, :] = dot_f32(hot_b, ys[b], 0, 0).astype(jnp.bfloat16)
        slot_grad = jnp.concatenate([part[b] for part in slot_grads], axis=0)
        gate = gates[b]
        grad_gate = [
            jnp.sum(
                jnp.where(slot_index == loc[b, k : k + 1, :], slot_grad, 0.0),
                axis=0,
                keepdims=True,
            )
            for k in range(top)
        ]
        centre = gate[0] * grad_gate[0]
        for k in range(1, top):
            centre = centre + gate[k] * grad_gate[k]
        grad_logits = jnp.zeros((experts, rows), jnp.float32)
        for k in range(top):
            grad_logits = jnp.where(
                expert_index == eid[b, k : k + 1, :],
                gate[k] * (grad_gate[k] - centre),
                grad_logits,
            )
        grad_logits = grad_logits.astype(jnp.bfloat16)
        dh2[b * rows : (b + 1) * rows, :] = (
            dot_f32(hot_b, ds[b], 0, 0) + dot_f32(grad_logits, router[...], 0, 0)
        ).astype(jnp.bfloat16)
        grad_rt[...] += dot_f32(grad_logits, h_blk, 1, 0)


def whole_spec():
    return pl.BlockSpec(memory_space=pltpu.VMEM)


def per_device_tokens(
    tokens,
    segment_ids,
    expert_ids,
    slot_ids,
    norm1_gain,
    w_query,
    w_key,
    w_value,
    w_out,
    norm2_gain,
    w_router,
    w_gate,
    w_up,
    w_down,
    cotangent,
):
    rows_dev, width = tokens.shape
    top = expert_ids.shape[1]
    experts = w_router.shape[1]
    cap = rows_dev * top // experts
    local_experts = w_gate.shape[0]
    hidden_width = w_gate.shape[2]
    length = segment_ids.shape[0]
    per_seq = length // rows_dev
    seqs = experts // local_experts
    q_width, k_width = w_query.shape[1], w_key.shape[1]
    bf16, f32 = jnp.bfloat16, jnp.float32
    params = pltpu.CompilerParams(vmem_limit_bytes=VMEM_BYTES)

    x_all_b = lax.all_gather(tokens, "tensor", axis=0, tiled=True)
    w_out_in, x_all_b = lax.optimization_barrier((w_out, x_all_b))
    w_out_all = lax.all_gather(w_out_in, "tensor", axis=0, tiled=True)
    cot_in, w_out_all = lax.optimization_barrier((cotangent, w_out_all))
    cot_seq = lax.all_gather(cot_in, "tensor", axis=0, tiled=True)
    cot_all = lax.all_gather(cot_seq, "expert", axis=0, tiled=True)
    code = (expert_ids * (cap + 1) + slot_ids + 1).T.reshape(1, top, rows_dev)
    code = lax.all_gather(code, "tensor", axis=0, tiled=True)
    code = lax.all_gather(code, "expert", axis=0, tiled=True)
    eid = code // (cap + 1)
    slot = code - eid * (cap + 1) - 1
    first_slot = lax.axis_index("expert") * (local_experts * cap)
    loc = jnp.where(slot >= 0, eid * cap + slot - first_slot, -1)
    w_gu = jnp.concatenate([w_gate, w_up], axis=2)
    router_t = w_router.T

    x_all = x_all_b.astype(f32)
    r1 = lax.rsqrt(jnp.mean(x_all * x_all, axis=-1, keepdims=True) + EPSILON)
    h1 = (x_all * r1 * norm1_gain).astype(bf16)
    cos_table, sine_table = rope_tables(jnp.arange(length).astype(f32), HDIM)
    cos_t = jnp.tile(cos_table[:, 0, :], (1, q_width // HDIM))
    sin_t = jnp.tile(sine_table[:, 0, :], (1, q_width // HDIM))
    seg_col, seg_row = segment_ids[:, None], segment_ids[None, :]
    q_raw = jnp.dot(h1, w_query, preferred_element_type=f32)
    k_raw = jnp.dot(h1, w_key, preferred_element_type=f32)
    values = jnp.dot(h1, w_value, preferred_element_type=f32).astype(bf16)
    heads_out, queries, keys = pl.pallas_call(
        attention_forward,
        out_shape=(
            jax.ShapeDtypeStruct((length, q_width), bf16),
            jax.ShapeDtypeStruct((length, q_width), bf16),
            jax.ShapeDtypeStruct((length, k_width), bf16),
        ),
        in_specs=[whole_spec()] * 7,
        out_specs=(whole_spec(),) * 3,
        compiler_params=params,
        cost_estimate=pl.CostEstimate(
            flops=6 * length * length * q_width, bytes_accessed=8 * length * q_width, transcendentals=length * length * 4
        ),
        name="attention_forward",
    )(q_raw, k_raw, values, cos_t, sin_t, seg_col, seg_row)
    heads_all = lax.all_gather(heads_out, "tensor", axis=1, tiled=True)
    y_all = x_all + RESIDUAL * jnp.dot(heads_all, w_out_all, preferred_element_type=f32)
    r2_all = lax.rsqrt(jnp.mean(y_all * y_all, axis=-1, keepdims=True) + EPSILON)
    h2_seq = (y_all * r2_all * norm2_gain).astype(bf16)
    h2_all = lax.all_gather(h2_seq, "expert", axis=0, tiled=True)

    slots = local_experts * cap
    total_rows = seqs * length
    moe_part, dh2_part, grad_gu, grad_dn, grad_rt = pl.pallas_call(
        expert_kernel,
        grid=(seqs,),
        out_shape=(
            jax.ShapeDtypeStruct((total_rows, width), bf16),
            jax.ShapeDtypeStruct((total_rows, width), bf16),
            jax.ShapeDtypeStruct((local_experts, width, 2 * hidden_width), f32),
            jax.ShapeDtypeStruct((local_experts, hidden_width, width), f32),
            jax.ShapeDtypeStruct((experts, width), f32),
        ),
        in_specs=[
            pl.BlockSpec((length, width), lambda i: (i, 0)),
            pl.BlockSpec((length, width), lambda i: (i, 0)),
            pl.BlockSpec((per_seq, top, rows_dev), lambda i: (i, 0, 0)),
            pl.BlockSpec((per_seq, top, rows_dev), lambda i: (i, 0, 0)),
            pl.BlockSpec((experts, width), lambda i: (0, 0)),
            pl.BlockSpec((local_experts, width, 2 * hidden_width), lambda i: (0, 0, 0)),
            pl.BlockSpec((local_experts, hidden_width, width), lambda i: (0, 0, 0)),
        ],
        out_specs=(
            pl.BlockSpec((length, width), lambda i: (i, 0)),
            pl.BlockSpec((length, width), lambda i: (i, 0)),
            pl.BlockSpec((local_experts, width, 2 * hidden_width), lambda i: (0, 0, 0)),
            pl.BlockSpec((local_experts, hidden_width, width), lambda i: (0, 0, 0)),
            pl.BlockSpec((experts, width), lambda i: (0, 0)),
        ),
        scratch_shapes=[
            pltpu.VMEM((per_seq, slots, width), bf16),
            pltpu.VMEM((per_seq, slots, width), bf16),
            pltpu.VMEM((per_seq, slots, width), bf16),
            pltpu.VMEM((per_seq, slots, width), bf16),
            pltpu.VMEM((per_seq, slots, rows_dev), bf16),
            pltpu.VMEM((per_seq, slots, 1), f32),
        ],
        compiler_params=params,
        cost_estimate=pl.CostEstimate(
            flops=40 * 10**9, bytes_accessed=8 * total_rows * width, transcendentals=0
        ),
        name="experts",
    )(h2_all, cot_all, eid, loc, router_t, w_gu, w_down)

    dh2 = lax.psum_scatter(dh2_part, "expert", scatter_dimension=0, tiled=True)
    moe_in, dh2 = lax.optimization_barrier((moe_part, dh2))
    dh2 = lax.psum_scatter(dh2, "tensor", scatter_dimension=0, tiled=True).astype(f32)
    moe = lax.psum_scatter(moe_in, "expert", scatter_dimension=0, tiled=True)

    row_start = lax.axis_index("tensor") * rows_dev
    y_own = lax.dynamic_slice_in_dim(y_all, row_start, rows_dev, 0)
    r2 = lax.rsqrt(jnp.mean(y_own * y_own, axis=-1, keepdims=True) + EPSILON)
    n2 = y_own * r2
    upstream = cotangent.astype(f32)
    grad_norm2 = jnp.sum(dh2 * n2, axis=0)
    dn = dh2 * norm2_gain
    dy = upstream + r2 * (dn - n2 * jnp.mean(dn * n2, axis=-1, keepdims=True))
    grad_attn = lax.all_gather((RESIDUAL * dy).astype(bf16), "tensor", axis=0, tiled=True)
    moe_late, grad_attn = lax.optimization_barrier((moe, grad_attn))
    moe_own = lax.psum_scatter(moe_late, "tensor", scatter_dimension=0, tiled=True).astype(f32)
    mixed = (y_own + RESIDUAL * moe_own).astype(bf16)
    grad_rt = lax.psum(grad_rt, ("expert", "tensor"))

    grad_heads = dot_f32(grad_attn, w_out, 1, 1).astype(bf16)
    grad_out_w = contract_rows(heads_out, grad_attn).astype(bf16)
    dq_raw, dk_raw, dv_raw = pl.pallas_call(
        attention_backward,
        out_shape=(
            jax.ShapeDtypeStruct((length, q_width), bf16),
            jax.ShapeDtypeStruct((length, k_width), bf16),
            jax.ShapeDtypeStruct((length, k_width), bf16),
        ),
        in_specs=[whole_spec()] * 8,
        out_specs=(whole_spec(),) * 3,
        scratch_shapes=[
            pltpu.VMEM((length, q_width), f32),
            pltpu.VMEM((length, k_width), f32),
            pltpu.VMEM((length, k_width), f32),
        ],
        compiler_params=params,
        cost_estimate=pl.CostEstimate(
            flops=12 * length * length * q_width, bytes_accessed=8 * length * q_width, transcendentals=length * length * 4
        ),
        name="attention_backward",
    )(queries, keys, values, grad_heads, cos_t, sin_t, seg_col, seg_row)
    summed = dot_f32(dq_raw, w_query, 1, 1) + dot_f32(dk_raw, w_key, 1, 1)
    summed = summed + dot_f32(dv_raw, w_value, 1, 1)
    dh1 = lax.psum_scatter(
        summed.astype(bf16), "tensor", scatter_dimension=0, tiled=True
    ).astype(f32)
    grad_norm1 = jnp.sum(summed * (x_all * r1), axis=0)
    grad_norm1, grad_norm2 = lax.psum((grad_norm1, grad_norm2), ("expert", "tensor"))
    grad_q, grad_k, grad_v, grad_out_w = lax.psum(
        (
            contract_rows(h1, dq_raw).astype(bf16),
            contract_rows(h1, dk_raw).astype(bf16),
            contract_rows(h1, dv_raw).astype(bf16),
            grad_out_w,
        ),
        "expert",
    )
    x_own = tokens.astype(f32)
    r1_own = lax.rsqrt(jnp.mean(x_own * x_own, axis=-1, keepdims=True) + EPSILON)
    n1 = x_own * r1_own
    dn1 = dh1 * norm1_gain
    grad_input = dy + r1_own * (dn1 - n1 * jnp.mean(dn1 * n1, axis=-1, keepdims=True))
    return (
        mixed,
        grad_input,
        grad_norm1,
        grad_q.astype(f32),
        grad_k.astype(f32),
        grad_v.astype(f32),
        grad_out_w.astype(f32),
        grad_norm2,
        grad_rt.T,
        grad_gu[:, :, :hidden_width],
        grad_gu[:, :, hidden_width:],
        grad_dn,
    )


def choose_plan(mesh):
    def per_device(tokens, *rest):
        gathered = tokens.size * 2 * mesh.shape["expert"] * mesh.shape["tensor"]
        plan = per_device_tokens if gathered <= GATHER_LIMIT else per_device_slots
        return plan(tokens, *rest)

    return per_device


def solution(mesh):
    return jax.shard_map(
        choose_plan(mesh),
        mesh=mesh,
        in_specs=(
            P(("expert", "tensor"), None),
            P("expert"),
            P(("expert", "tensor"), None),
            P(("expert", "tensor"), None),
            P(),
            P(None, "tensor"),
            P(None, "tensor"),
            P(None, "tensor"),
            P("tensor", None),
            P(),
            P(),
            P("expert", None, "tensor"),
            P("expert", None, "tensor"),
            P("expert", "tensor", None),
            P(("expert", "tensor"), None),
        ),
        out_specs=(
            P(("expert", "tensor"), None),
            P(("expert", "tensor"), None),
            P(),
            P(None, "tensor"),
            P(None, "tensor"),
            P(None, "tensor"),
            P("tensor", None),
            P(),
            P(),
            P("expert", None, "tensor"),
            P("expert", None, "tensor"),
            P("expert", "tensor", None),
        ),
        check_vma=False,
    )
```

```python
import jax
import jax.numpy as jnp
from jax import lax
from jax.experimental import pallas as pl
from jax.experimental.pallas import tpu as pltpu
from jax.sharding import PartitionSpec as P

HDIM = 64


EPSILON = 1e-06
RESIDUAL = 0.22
MASKED = -1e30
ATTENTION_MULTIPLIER = 0.015625


def normed(rows, gain):
    return rows * lax.rsqrt(jnp.mean(rows * rows, axis=-1, keepdims=True) + EPSILON) * gain


def rope_tables(positions, width):
    half_width = width // 2
    frequency = 10000.0 ** (-(jnp.arange(half_width, dtype=jnp.float32) * 2.0) / width)
    angles = positions[:, None] * frequency[None, :]
    cos_table = jnp.concatenate([jnp.cos(angles), jnp.cos(angles)], axis=-1)
    sine_table = jnp.concatenate([jnp.sin(angles), jnp.sin(angles)], axis=-1)
    return (cos_table[:, None, :], sine_table[:, None, :])


def rotate(head_vals, cos_table, sine_table):
    half_width = head_vals.shape[-1] // 2
    turned = jnp.concatenate([-head_vals[..., half_width:], head_vals[..., :half_width]], axis=-1)
    return head_vals * cos_table + turned * sine_table


def contract_rows(left, right):
    return lax.dot_general(
        left, right, (((0,), (0,)), ((), ())), preferred_element_type=jnp.float32
    )


def contract_cols(left, right):
    return lax.dot_general(
        left, right, (((1,), (1,)), ((), ())), preferred_element_type=jnp.float32
    )


def per_device_slots(
    tokens,
    segment_ids,
    expert_ids,
    slot_ids,
    norm1_gain,
    w_query,
    w_key,
    w_value,
    w_out,
    norm2_gain,
    w_router,
    w_gate,
    w_up,
    w_down,
    cotangent,
):
    rows_dev, model_width = tokens.shape
    top_count = expert_ids.shape[1]
    experts = w_router.shape[1]
    capacity = rows_dev * top_count // experts
    head_dim = HDIM
    key_heads = w_key.shape[1] // head_dim
    query_heads = w_query.shape[1] // head_dim
    group_size = query_heads // key_heads
    score_scale = ATTENTION_MULTIPLIER
    length = segment_ids.shape[0]
    block_rows = min(length, 512)
    blocks = length // block_rows
    inputs_f = tokens.astype(jnp.float32)
    normed_one_f, norm_one_back = jax.vjp(normed, inputs_f, norm1_gain)
    normed_one = normed_one_f.astype(jnp.bfloat16)
    whole_rows = lax.all_gather(normed_one, "tensor", axis=0, tiled=True)
    cos_table, sine_table = rope_tables(jnp.arange(length).astype(jnp.float32), head_dim)
    query_raw = jnp.dot(whole_rows, w_query, preferred_element_type=jnp.float32).reshape(
        length, query_heads, head_dim
    )
    key_raw = jnp.dot(whole_rows, w_key, preferred_element_type=jnp.float32).reshape(
        length, key_heads, head_dim
    )
    queries = (
        rotate(query_raw, cos_table, sine_table)
        .astype(jnp.bfloat16)
        .reshape(length, key_heads, group_size, head_dim)
    )
    keys_all = rotate(key_raw, cos_table, sine_table).astype(jnp.bfloat16)
    values_all = (
        jnp.dot(whole_rows, w_value, preferred_element_type=jnp.float32)
        .astype(jnp.bfloat16)
        .reshape(length, key_heads, head_dim)
    )
    key_index = jnp.arange(length)

    def scores(query_block, row_start):
        row_index = row_start + jnp.arange(block_rows)
        seg_rows = lax.dynamic_slice_in_dim(segment_ids, row_start, block_rows)
        allowed = (row_index[:, None] >= key_index[None, :]) & (
            seg_rows[:, None] == segment_ids[None, :]
        )
        raw_scores = (
            jnp.einsum("qkgd,skd->kgqs", query_block, keys_all, preferred_element_type=jnp.float32)
            * score_scale
        )
        return jnp.where(allowed[None, None], raw_scores, MASKED)

    query_blocks = queries.reshape(blocks, block_rows, key_heads, group_size, head_dim)
    row_starts = jnp.arange(blocks, dtype=jnp.int32) * block_rows

    def forward_block(block_items):
        query_block, row_start = block_items
        logits = scores(query_block, row_start)
        peak_score = jnp.max(logits, axis=-1, keepdims=True)
        weights = jnp.exp(logits - peak_score)
        row_total = jnp.sum(weights, axis=-1, keepdims=True)
        probability = (weights / row_total).astype(jnp.bfloat16)
        mixed_heads = jnp.einsum(
            "kgqs,skd->qkgd", probability, values_all, preferred_element_type=jnp.float32
        )
        return (mixed_heads.astype(jnp.bfloat16), (peak_score + jnp.log(row_total))[..., 0])

    head_out, log_totals = lax.map(forward_block, (query_blocks, row_starts))
    head_out = head_out.reshape(length, query_heads * head_dim)
    row_part = head_out
    attn = lax.psum_scatter(
        jnp.dot(row_part, w_out, preferred_element_type=jnp.float32),
        "tensor",
        scatter_dimension=0,
        tiled=True,
    )
    residual = inputs_f + RESIDUAL * attn
    normed_two_f, norm_two_back = jax.vjp(normed, residual, norm2_gain)
    normed_two = normed_two_f.astype(jnp.bfloat16)
    router_logits = jnp.dot(normed_two, w_router, preferred_element_type=jnp.float32)
    selector = (expert_ids[:, :, None] == jnp.arange(experts)[None, None, :]).astype(jnp.float32)

    def gating(logit_rows):
        return jax.nn.softmax(jnp.sum(selector * logit_rows[:, None, :], axis=-1), axis=-1)

    gate_weights, gating_back = jax.vjp(gating, router_logits)
    target = jnp.where(slot_ids >= 0, expert_ids * capacity + slot_ids, -1).reshape(
        rows_dev * top_count
    )
    onehot = (target[:, None] == jnp.arange(experts * capacity)[None, :]).astype(jnp.bfloat16)
    row_hot = jnp.sum(onehot.reshape(rows_dev, top_count, experts * capacity), axis=1)
    outgoing = (
        contract_rows(row_hot, normed_two)
        .astype(jnp.bfloat16)
        .reshape(experts, capacity, model_width)
    )
    arrived = lax.all_to_all(outgoing, "expert", split_axis=0, concat_axis=1, tiled=True)
    gate_w, up_w, down_w = (
        lax.all_gather(w_gate, "tensor", axis=2, tiled=True),
        lax.all_gather(w_up, "tensor", axis=2, tiled=True),
        lax.all_gather(w_down, "tensor", axis=1, tiled=True),
    )
    gate_act = jnp.einsum("erd,edf->erf", arrived, gate_w, preferred_element_type=jnp.float32)
    up_act = jnp.einsum("erd,edf->erf", arrived, up_w, preferred_element_type=jnp.float32)
    sigmoid_gate = jax.nn.sigmoid(gate_act)
    swish_act = gate_act * sigmoid_gate
    hidden = (swish_act * up_act).astype(jnp.bfloat16)
    expert_terms = jnp.einsum("erf,efd->erd", hidden, down_w, preferred_element_type=jnp.float32)
    returned = lax.all_to_all(
        expert_terms.astype(jnp.bfloat16), "expert", split_axis=1, concat_axis=0, tiled=True
    )
    picked = jnp.dot(
        onehot,
        returned.reshape(experts * capacity, model_width),
        preferred_element_type=jnp.float32,
    )
    picked = picked.reshape(rows_dev, top_count, model_width)
    expert_mix = jnp.sum(gate_weights[:, :, None] * picked, axis=1)
    mixed_out = (residual + RESIDUAL * expert_mix).astype(jnp.bfloat16)
    upstream = cotangent.astype(jnp.float32)
    grad_mix = RESIDUAL * upstream
    grad_gates = jnp.sum(picked * grad_mix[:, None, :], axis=-1)
    grad_picked = (
        (gate_weights[:, :, None] * grad_mix[:, None, :])
        .astype(jnp.bfloat16)
        .reshape(rows_dev * top_count, model_width)
    )
    grad_slots = (
        contract_rows(onehot, grad_picked)
        .astype(jnp.bfloat16)
        .reshape(experts, capacity, model_width)
    )
    grad_arrived = lax.all_to_all(grad_slots, "expert", split_axis=0, concat_axis=1, tiled=True)
    grad_down_w = jnp.einsum(
        "erf,erd->efd", hidden, grad_arrived, preferred_element_type=jnp.float32
    )
    grad_hidden = jnp.einsum(
        "erd,efd->erf", grad_arrived, down_w, preferred_element_type=jnp.float32
    )
    grad_gate_act = (
        grad_hidden * up_act * (sigmoid_gate * (1.0 + gate_act * (1.0 - sigmoid_gate)))
    ).astype(jnp.bfloat16)
    grad_up_act = (grad_hidden * swish_act).astype(jnp.bfloat16)
    grad_gate_w = jnp.einsum(
        "erd,erf->edf", arrived, grad_gate_act, preferred_element_type=jnp.float32
    )
    grad_up_w = jnp.einsum("erd,erf->edf", arrived, grad_up_act, preferred_element_type=jnp.float32)
    grad_rows_in = jnp.einsum(
        "erf,edf->erd", grad_gate_act, gate_w, preferred_element_type=jnp.float32
    )
    grad_rows_in = grad_rows_in + jnp.einsum(
        "erf,edf->erd", grad_up_act, up_w, preferred_element_type=jnp.float32
    )
    grad_gate_w, grad_up_w, grad_down_w = (
        lax.psum_scatter(
            grad_gate_w.astype(jnp.bfloat16), "tensor", scatter_dimension=2, tiled=True
        ).astype(jnp.float32),
        lax.psum_scatter(
            grad_up_w.astype(jnp.bfloat16), "tensor", scatter_dimension=2, tiled=True
        ).astype(jnp.float32),
        lax.psum_scatter(
            grad_down_w.astype(jnp.bfloat16), "tensor", scatter_dimension=1, tiled=True
        ).astype(jnp.float32),
    )
    grad_returned = lax.all_to_all(
        grad_rows_in.astype(jnp.bfloat16), "expert", split_axis=1, concat_axis=0, tiled=True
    )
    grad_normed_two = jnp.dot(
        onehot,
        grad_returned.reshape(experts * capacity, model_width),
        preferred_element_type=jnp.float32,
    )
    grad_normed_two = jnp.sum(grad_normed_two.reshape(rows_dev, top_count, model_width), axis=1)
    grad_logits = gating_back(grad_gates)[0].astype(jnp.bfloat16)
    grad_router = contract_rows(normed_two, grad_logits)
    grad_normed_two = grad_normed_two + contract_cols(grad_logits, w_router)
    grad_residual, grad_norm2 = norm_two_back(grad_normed_two)
    grad_residual = grad_residual + upstream
    grad_attn = (RESIDUAL * grad_residual).astype(jnp.bfloat16)
    grad_attn_all = lax.all_gather(grad_attn, "tensor", axis=0, tiled=True)
    grad_out_w = contract_rows(head_out, grad_attn_all)
    grad_heads = contract_cols(grad_attn_all, w_out).astype(jnp.bfloat16)
    grad_heads = grad_heads.reshape(blocks, block_rows, key_heads, group_size, head_dim)

    def backward_block(carried, block_items):
        grad_keys, grad_values = carried
        query_block, row_start, log_total, grad_block = block_items
        logits = scores(query_block, row_start)
        probability = jnp.exp(logits - log_total[..., None])
        grad_values = grad_values + jnp.einsum(
            "kgqs,qkgd->skd",
            probability.astype(jnp.bfloat16),
            grad_block,
            preferred_element_type=jnp.float32,
        )
        grad_probs = jnp.einsum(
            "qkgd,skd->kgqs", grad_block, values_all, preferred_element_type=jnp.float32
        )
        centre = jnp.sum(probability * grad_probs, axis=-1, keepdims=True)
        grad_scores = (probability * (grad_probs - centre)).astype(jnp.bfloat16)
        grad_query_block = (
            jnp.einsum("kgqs,skd->qkgd", grad_scores, keys_all, preferred_element_type=jnp.float32)
            * score_scale
        )
        grad_keys = (
            grad_keys
            + jnp.einsum(
                "kgqs,qkgd->skd", grad_scores, query_block, preferred_element_type=jnp.float32
            )
            * score_scale
        )
        return ((grad_keys, grad_values), grad_query_block)

    zero_keys = jnp.zeros((length, key_heads, head_dim), jnp.float32)
    (grad_keys, grad_values), grad_queries = lax.scan(
        backward_block, (zero_keys, zero_keys), (query_blocks, row_starts, log_totals, grad_heads)
    )
    grad_queries = grad_queries.reshape(length, query_heads, head_dim)
    _, rope_query_back = jax.vjp(
        lambda head_vals: rotate(head_vals, cos_table, sine_table), query_raw
    )
    _, rope_key_back = jax.vjp(lambda head_vals: rotate(head_vals, cos_table, sine_table), key_raw)
    grad_query_raw = (
        rope_query_back(grad_queries)[0]
        .astype(jnp.bfloat16)
        .reshape(length, query_heads * head_dim)
    )
    grad_key_raw = (
        rope_key_back(grad_keys)[0].astype(jnp.bfloat16).reshape(length, key_heads * head_dim)
    )
    grad_value_raw = grad_values.astype(jnp.bfloat16).reshape(length, key_heads * head_dim)
    grad_query_w = contract_rows(whole_rows, grad_query_raw)
    grad_key_w = contract_rows(whole_rows, grad_key_raw)
    grad_value_w = contract_rows(whole_rows, grad_value_raw)

    def row_part(values_in):
        return values_in

    summed = contract_cols(row_part(grad_query_raw), w_query)
    summed = summed + contract_cols(row_part(grad_key_raw), w_key)
    grad_normed_one = lax.psum_scatter(
        (summed + contract_cols(row_part(grad_value_raw), w_value)).astype(jnp.bfloat16),
        "tensor",
        scatter_dimension=0,
        tiled=True,
    ).astype(jnp.float32)
    grad_inputs, grad_norm1 = norm_one_back(grad_normed_one)
    grad_inputs = grad_inputs + grad_residual
    grad_query_w, grad_key_w, grad_value_w, grad_out_w = (
        lax.psum(grad_query_w.astype(jnp.bfloat16), "expert").astype(jnp.float32),
        lax.psum(grad_key_w.astype(jnp.bfloat16), "expert").astype(jnp.float32),
        lax.psum(grad_value_w.astype(jnp.bfloat16), "expert").astype(jnp.float32),
        lax.psum(grad_out_w.astype(jnp.bfloat16), "expert").astype(jnp.float32),
    )
    grad_norm1, grad_norm2, grad_router = lax.psum(
        (grad_norm1, grad_norm2, grad_router), ("expert", "tensor")
    )
    return (
        mixed_out,
        grad_inputs,
        grad_norm1,
        grad_query_w,
        grad_key_w,
        grad_value_w,
        grad_out_w,
        grad_norm2,
        grad_router,
        grad_gate_w,
        grad_up_w,
        grad_down_w,
    )


ROW_BLOCK = 256
VMEM_BYTES = 58 * 1024 * 1024
GATHER_LIMIT = 32 * 1024 * 1024


def dot_f32(left, right, left_dim, right_dim):
    return lax.dot_general(
        left,
        right,
        (((left_dim,), (right_dim,)), ((), ())),
        preferred_element_type=jnp.float32,
    )


def half_swap(values):
    width = values.shape[-1]
    half = HDIM // 2
    lane = lax.broadcasted_iota(jnp.int32, values.shape, 1)
    ahead = pltpu.roll(values, width - half, 1)
    behind = pltpu.roll(values, half, 1)
    first = (lane % HDIM) < half
    return jnp.where(first, ahead, behind), first


def rope_rows(values, cos_table, sine_table):
    swapped, first = half_swap(values)
    return values * cos_table + jnp.where(first, -swapped, swapped) * sine_table


def rope_rows_back(values, cos_table, sine_table):
    swapped, first = half_swap(values * sine_table)
    return values * cos_table + jnp.where(first, swapped, -swapped)


def block_mask(seg_col, seg_row, start, rows, keys):
    row_index = start + lax.broadcasted_iota(jnp.int32, (rows, keys), 0)
    key_index = lax.broadcasted_iota(jnp.int32, (rows, keys), 1)
    return (row_index >= key_index) & (seg_col[start : start + rows, :] == seg_row[:, :keys])


def attention_forward(
    q_raw, k_raw, values, cos_t, sin_t, seg_col, seg_row, heads_out, queries, keys_out
):
    length, q_width = q_raw.shape
    k_width = k_raw.shape[1]
    queries[...] = rope_rows(q_raw[...], cos_t[...], sin_t[...]).astype(jnp.bfloat16)
    keys_out[...] = rope_rows(k_raw[...], cos_t[:, :k_width], sin_t[:, :k_width]).astype(
        jnp.bfloat16
    )
    group = q_width // k_width
    rows = min(length, ROW_BLOCK)
    for start in range(0, length, rows):
        count = start + rows
        allowed = block_mask(seg_col, seg_row, start, rows, count)
        for head in range(q_width // HDIM):
            kv = head // group
            q_blk = queries[start:count, head * HDIM : (head + 1) * HDIM]
            k_blk = keys_out[:count, kv * HDIM : (kv + 1) * HDIM]
            v_blk = values[:count, kv * HDIM : (kv + 1) * HDIM]
            score = dot_f32(q_blk, k_blk, 1, 1) * ATTENTION_MULTIPLIER
            score = jnp.where(allowed, score, MASKED)
            weight = jnp.exp(score - jnp.max(score, axis=1, keepdims=True))
            prob = weight * (1.0 / jnp.sum(weight, axis=1, keepdims=True))
            out = dot_f32(prob.astype(jnp.bfloat16), v_blk, 1, 0)
            heads_out[start:count, head * HDIM : (head + 1) * HDIM] = out.astype(jnp.bfloat16)


def attention_backward(
    queries, keys, values, grad_heads, cos_t, sin_t, seg_col, seg_row, dq_out, dk_out, dv_out, dq, dk, dv
):
    length, q_width = queries.shape
    k_width = keys.shape[1]
    group = q_width // k_width
    rows = min(length, ROW_BLOCK)
    dk[...] = jnp.zeros_like(dk)
    dv[...] = jnp.zeros_like(dv)
    for start in range(0, length, rows):
        count = start + rows
        allowed = block_mask(seg_col, seg_row, start, rows, count)
        for head in range(q_width // HDIM):
            kv = head // group
            q_blk = queries[start:count, head * HDIM : (head + 1) * HDIM]
            g_blk = grad_heads[start:count, head * HDIM : (head + 1) * HDIM]
            k_blk = keys[:count, kv * HDIM : (kv + 1) * HDIM]
            v_blk = values[:count, kv * HDIM : (kv + 1) * HDIM]
            score = dot_f32(q_blk, k_blk, 1, 1) * ATTENTION_MULTIPLIER
            score = jnp.where(allowed, score, MASKED)
            weight = jnp.exp(score - jnp.max(score, axis=1, keepdims=True))
            prob = weight * (1.0 / jnp.sum(weight, axis=1, keepdims=True))
            grad_prob = dot_f32(g_blk, v_blk, 1, 1)
            centre = jnp.sum(prob * grad_prob, axis=1, keepdims=True)
            grad_score = (prob * (grad_prob - centre)).astype(jnp.bfloat16)
            dq[start:count, head * HDIM : (head + 1) * HDIM] = (
                dot_f32(grad_score, k_blk, 1, 0) * ATTENTION_MULTIPLIER
            )
            dk[:count, kv * HDIM : (kv + 1) * HDIM] += dot_f32(grad_score, q_blk, 0, 0)
            dv[:count, kv * HDIM : (kv + 1) * HDIM] += dot_f32(
                prob.astype(jnp.bfloat16), g_blk, 0, 0
            )
    dq_out[...] = rope_rows_back(dq[...], cos_t[...], sin_t[...]).astype(jnp.bfloat16)
    dk_out[...] = rope_rows_back(
        dk[...] * ATTENTION_MULTIPLIER, cos_t[:, :k_width], sin_t[:, :k_width]
    ).astype(jnp.bfloat16)
    dv_out[...] = dv[...].astype(jnp.bfloat16)


def expert_kernel(
    h2, dz, eid, loc, router, w_gu, w_dn, moe, dh2, grad_gu, grad_dn, grad_rt, xs, zs, ys, ds, hot, gate_s
):
    blocks, top, rows = eid.shape
    experts = router.shape[0]
    local_experts, _, double_hidden = w_gu.shape
    hidden_width = double_hidden // 2
    slots = hot.shape[1]
    cap = slots // local_experts

    @pl.when(pl.program_id(0) == 0)
    def _():
        grad_gu[...] = jnp.zeros_like(grad_gu)
        grad_dn[...] = jnp.zeros_like(grad_dn)
        grad_rt[...] = jnp.zeros_like(grad_rt)

    slot_index = lax.broadcasted_iota(jnp.int32, (slots, rows), 0)
    expert_index = lax.broadcasted_iota(jnp.int32, (experts, rows), 0)
    gates = []
    for b in range(blocks):
        h_blk = h2[b * rows : (b + 1) * rows, :]
        z_blk = dz[b * rows : (b + 1) * rows, :]
        logits = dot_f32(router[...], h_blk, 1, 1)
        chosen = [
            jnp.sum(
                jnp.where(expert_index == eid[b, k : k + 1, :], logits, 0.0), axis=0, keepdims=True
            )
            for k in range(top)
        ]
        peak = chosen[0]
        for k in range(1, top):
            peak = jnp.maximum(peak, chosen[k])
        powers = [jnp.exp(c - peak) for c in chosen]
        total = powers[0]
        for k in range(1, top):
            total = total + powers[k]
        gate = [p / total for p in powers]
        gates.append(gate)
        weighted = jnp.zeros((slots, rows), jnp.float32)
        chosen_hot = jnp.zeros((slots, rows), jnp.float32)
        for k in range(top):
            hit = slot_index == loc[b, k : k + 1, :]
            weighted = jnp.where(hit, gate[k], weighted)
            chosen_hot = jnp.where(hit, 1.0, chosen_hot)
        hot_b = chosen_hot.astype(jnp.bfloat16)
        hot[b] = hot_b
        gate_s[b] = jnp.sum(weighted, axis=1, keepdims=True)
        xs[b] = dot_f32(hot_b, h_blk, 1, 0).astype(jnp.bfloat16)
        zs[b] = dot_f32(hot_b, z_blk, 1, 0).astype(jnp.bfloat16)
    slot_grads = []
    for e in range(local_experts):
        span = slice(e * cap, (e + 1) * cap)
        x_e = xs[:, span, :].reshape(blocks * cap, -1)
        z_e = zs[:, span, :].reshape(blocks * cap, -1)
        gate_e = gate_s[:, span, :].reshape(blocks * cap, 1)
        both = dot_f32(x_e, w_gu[e], 1, 0)
        g_act, u_act = both[:, :hidden_width], both[:, hidden_width:]
        sig = 1.0 / (1.0 + jnp.exp(-g_act))
        swish = g_act * sig
        hid_f = swish * u_act
        hid = hid_f.astype(jnp.bfloat16)
        out = dot_f32(hid, w_dn[e], 1, 0)
        ys[:, span, :] = (gate_e * out).astype(jnp.bfloat16).reshape(blocks, cap, -1)
        grad_raw = dot_f32(z_e, w_dn[e], 1, 1) * RESIDUAL
        slot_grads.append(
            jnp.sum(hid.astype(jnp.float32) * grad_raw, axis=1, keepdims=True).reshape(
                blocks, cap, 1
            )
        )
        grad_hid = gate_e * grad_raw
        dg = grad_hid * u_act * (sig * (1.0 + g_act * (1.0 - sig)))
        du = grad_hid * swish
        dgu = jnp.concatenate([dg, du], axis=1).astype(jnp.bfloat16)
        scaled = (hid.astype(jnp.float32) * (gate_e * RESIDUAL)).astype(jnp.bfloat16)
        grad_dn[e] += dot_f32(scaled, z_e, 0, 0)
        grad_gu[e] += dot_f32(x_e, dgu, 0, 0)
        ds[:, span, :] = dot_f32(dgu, w_gu[e], 1, 1).astype(jnp.bfloat16).reshape(blocks, cap, -1)
    for b in range(blocks):
        h_blk = h2[b * rows : (b + 1) * rows, :]
        hot_b = hot[b]
        moe[b * rows : (b + 1) * rows, :] = dot_f32(hot_b, ys[b], 0, 0).astype(jnp.bfloat16)
        slot_grad = jnp.concatenate([part[b] for part in slot_grads], axis=0)
        gate = gates[b]
        grad_gate = [
            jnp.sum(
                jnp.where(slot_index == loc[b, k : k + 1, :], slot_grad, 0.0),
                axis=0,
                keepdims=True,
            )
            for k in range(top)
        ]
        centre = gate[0] * grad_gate[0]
        for k in range(1, top):
            centre = centre + gate[k] * grad_gate[k]
        grad_logits = jnp.zeros((experts, rows), jnp.float32)
        for k in range(top):
            grad_logits = jnp.where(
                expert_index == eid[b, k : k + 1, :],
                gate[k] * (grad_gate[k] - centre),
                grad_logits,
            )
        grad_logits = grad_logits.astype(jnp.bfloat16)
        dh2[b * rows : (b + 1) * rows, :] = (
            dot_f32(hot_b, ds[b], 0, 0) + dot_f32(grad_logits, router[...], 0, 0)
        ).astype(jnp.bfloat16)
        grad_rt[...] += dot_f32(grad_logits, h_blk, 1, 0)


def whole_spec():
    return pl.BlockSpec(memory_space=pltpu.VMEM)


def per_device_tokens(
    tokens,
    segment_ids,
    expert_ids,
    slot_ids,
    norm1_gain,
    w_query,
    w_key,
    w_value,
    w_out,
    norm2_gain,
    w_router,
    w_gate,
    w_up,
    w_down,
    cotangent,
):
    rows_dev, width = tokens.shape
    top = expert_ids.shape[1]
    experts = w_router.shape[1]
    cap = rows_dev * top // experts
    local_experts = w_gate.shape[0]
    hidden_width = w_gate.shape[2]
    length = segment_ids.shape[0]
    per_seq = length // rows_dev
    seqs = experts // local_experts
    q_width, k_width = w_query.shape[1], w_key.shape[1]
    bf16, f32 = jnp.bfloat16, jnp.float32
    params = pltpu.CompilerParams(vmem_limit_bytes=VMEM_BYTES)

    tensors = per_seq
    mine = lax.axis_index("tensor")
    lane, place = mine % 2, mine // 2

    def shifted(block, step):
        return lax.ppermute(block, "tensor", [(i, (i + step) % tensors) for i in range(tensors)])

    def weight_partner(block):
        return lax.ppermute(block, "tensor", [(i, i ^ 1) for i in range(tensors)])

    def token_partner(block):
        return lax.ppermute(block, "tensor", [(i, i ^ 2) for i in range(tensors)])

    def token_pair(block):
        other = token_partner(block)
        first = jnp.where(place == 0, block, other)
        return jnp.concatenate([first, jnp.where(place == 0, other, block)], axis=0)

    def gather_rows(block):
        rows = block.shape[0]
        parts = [shifted(block, step) for step in range(1, tensors)]
        whole = jnp.zeros((tensors * rows, block.shape[1]), block.dtype)
        for step, part in enumerate([block] + parts):
            start = ((mine + tensors - step) % tensors) * rows
            whole = lax.dynamic_update_slice_in_dim(whole, part, start, 0)
        return whole

    code = (expert_ids * (cap + 1) + slot_ids + 1).T.reshape(1, top, rows_dev)
    code = lax.all_gather(token_pair(code), "expert", axis=0, tiled=True)
    x_all_b = lax.all_gather(tokens, "tensor", axis=0, tiled=True)
    cot_pair = token_pair(cotangent)
    w_out_in, cot_pair, code, x_all_b = lax.optimization_barrier((w_out, cot_pair, code, x_all_b))
    w_out_all = gather_rows(w_out_in)
    cot_all = lax.all_gather(cot_pair, "expert", axis=0, tiled=True)
    eid = code // (cap + 1)
    slot = code - eid * (cap + 1) - 1
    first_slot = lax.axis_index("expert") * (local_experts * cap)
    loc = jnp.where(slot >= 0, eid * cap + slot - first_slot, -1)
    router_t = w_router.T

    x_all = x_all_b.astype(f32)
    r1 = lax.rsqrt(jnp.mean(x_all * x_all, axis=-1, keepdims=True) + EPSILON)
    h1 = (x_all * r1 * norm1_gain).astype(bf16)
    cos_table, sine_table = rope_tables(jnp.arange(length).astype(f32), HDIM)
    cos_t = jnp.tile(cos_table[:, 0, :], (1, q_width // HDIM))
    sin_t = jnp.tile(sine_table[:, 0, :], (1, q_width // HDIM))
    seg_col, seg_row = segment_ids[:, None], segment_ids[None, :]
    q_raw = jnp.dot(h1, w_query, preferred_element_type=f32)
    k_raw = jnp.dot(h1, w_key, preferred_element_type=f32)
    values = jnp.dot(h1, w_value, preferred_element_type=f32).astype(bf16)
    heads_out, queries, keys = pl.pallas_call(
        attention_forward,
        out_shape=(
            jax.ShapeDtypeStruct((length, q_width), bf16),
            jax.ShapeDtypeStruct((length, q_width), bf16),
            jax.ShapeDtypeStruct((length, k_width), bf16),
        ),
        in_specs=[whole_spec()] * 7,
        out_specs=(whole_spec(),) * 3,
        compiler_params=params,
        cost_estimate=pl.CostEstimate(
            flops=6 * length * length * q_width, bytes_accessed=8 * length * q_width, transcendentals=length * length * 4
        ),
        name="attention_forward",
    )(q_raw, k_raw, values, cos_t, sin_t, seg_col, seg_row)
    heads_in, cot_all = lax.optimization_barrier((heads_out, cot_all))
    heads_all = lax.all_gather(heads_in, "tensor", axis=1, tiled=True)
    gate_in, up_in, down_in, heads_all, w_out_all = lax.optimization_barrier(
        (w_gate, w_up, w_down, heads_all, w_out_all)
    )
    w_gu = jnp.concatenate(
        [w_gate, weight_partner(gate_in), w_up, weight_partner(up_in)], axis=2
    )
    w_dn = jnp.concatenate([w_down, weight_partner(down_in)], axis=1)
    y_all = x_all + RESIDUAL * jnp.dot(heads_all, w_out_all, preferred_element_type=f32)
    r2_all = lax.rsqrt(jnp.mean(y_all * y_all, axis=-1, keepdims=True) + EPSILON)
    h2_seq = (y_all * r2_all * norm2_gain).astype(bf16)
    h2_pair = lax.dynamic_index_in_dim(
        h2_seq.reshape(2, 2, rows_dev, width), lane, 1, keepdims=False
    ).reshape(2 * rows_dev, width)
    h2_all = lax.all_gather(h2_pair, "expert", axis=0, tiled=True)

    slots = local_experts * cap
    total_rows = seqs * 2 * rows_dev
    per_step = per_seq
    step_rows = per_step * rows_dev
    wide = 2 * hidden_width
    once = pl.Buffered(1)
    moe_part, dh2_part, grad_gu, grad_dn, grad_rt = pl.pallas_call(
        expert_kernel,
        grid=(total_rows // step_rows,),
        out_shape=(
            jax.ShapeDtypeStruct((total_rows, width), bf16),
            jax.ShapeDtypeStruct((total_rows, width), bf16),
            jax.ShapeDtypeStruct((local_experts, width, 2 * wide), f32),
            jax.ShapeDtypeStruct((local_experts, wide, width), f32),
            jax.ShapeDtypeStruct((experts, width), f32),
        ),
        in_specs=[
            pl.BlockSpec((step_rows, width), lambda i: (i, 0)),
            pl.BlockSpec((step_rows, width), lambda i: (i, 0)),
            pl.BlockSpec((per_step, top, rows_dev), lambda i: (i, 0, 0)),
            pl.BlockSpec((per_step, top, rows_dev), lambda i: (i, 0, 0)),
            pl.BlockSpec((experts, width), lambda i: (0, 0)),
            pl.BlockSpec((local_experts, width, 2 * wide), lambda i: (0, 0, 0), pipeline_mode=once),
            pl.BlockSpec((local_experts, wide, width), lambda i: (0, 0, 0), pipeline_mode=once),
        ],
        out_specs=(
            pl.BlockSpec((step_rows, width), lambda i: (i, 0)),
            pl.BlockSpec((step_rows, width), lambda i: (i, 0)),
            pl.BlockSpec((local_experts, width, 2 * wide), lambda i: (0, 0, 0), pipeline_mode=once),
            pl.BlockSpec((local_experts, wide, width), lambda i: (0, 0, 0), pipeline_mode=once),
            pl.BlockSpec((experts, width), lambda i: (0, 0)),
        ),
        scratch_shapes=[
            pltpu.VMEM((per_seq, slots, width), bf16),
            pltpu.VMEM((per_seq, slots, width), bf16),
            pltpu.VMEM((per_seq, slots, width), bf16),
            pltpu.VMEM((per_seq, slots, width), bf16),
            pltpu.VMEM((per_seq, slots, rows_dev), bf16),
            pltpu.VMEM((per_seq, slots, 1), f32),
        ],
        compiler_params=params,
        cost_estimate=pl.CostEstimate(
            flops=40 * 10**9, bytes_accessed=8 * total_rows * width, transcendentals=0
        ),
        name="experts",
    )(h2_all, cot_all, eid, loc, router_t, w_gu, w_dn)

    def own_rows(pair):
        kept = lax.dynamic_slice_in_dim(pair, place * rows_dev, rows_dev, 0)
        sent = lax.dynamic_slice_in_dim(pair, (1 - place) * rows_dev, rows_dev, 0)
        return kept.astype(f32) + token_partner(sent).astype(f32)

    dh2_pair = lax.psum_scatter(dh2_part, "expert", scatter_dimension=0, tiled=True)
    moe_in, grad_rt, grad_gu, grad_dn, dh2_pair = lax.optimization_barrier(
        (moe_part, grad_rt, grad_gu, grad_dn, dh2_pair)
    )
    dh2 = own_rows(dh2_pair)
    moe_pair = lax.psum_scatter(moe_in, "expert", scatter_dimension=0, tiled=True)

    row_start = lax.axis_index("tensor") * rows_dev
    y_own = lax.dynamic_slice_in_dim(y_all, row_start, rows_dev, 0)
    r2 = lax.rsqrt(jnp.mean(y_own * y_own, axis=-1, keepdims=True) + EPSILON)
    n2 = y_own * r2
    upstream = cotangent.astype(f32)
    grad_norm2 = jnp.sum(dh2 * n2, axis=0)
    dn = dh2 * norm2_gain
    dy = upstream + r2 * (dn - n2 * jnp.mean(dn * n2, axis=-1, keepdims=True))
    grad_attn = gather_rows((RESIDUAL * dy).astype(bf16))
    small = lax.psum(jnp.concatenate([grad_rt, grad_norm2[None, :]], axis=0), "expert")
    small = lax.psum(small, "tensor")
    grad_rt, grad_norm2 = small[:experts], small[experts]
    gu_in, dn_in, grad_attn = lax.optimization_barrier((grad_gu, grad_dn, grad_attn))
    grad_gate = gu_in[:, :, :hidden_width] + weight_partner(
        gu_in[:, :, hidden_width:wide].astype(bf16)
    ).astype(f32)
    grad_up = gu_in[:, :, wide : wide + hidden_width] + weight_partner(
        gu_in[:, :, wide + hidden_width :].astype(bf16)
    ).astype(f32)
    grad_down = dn_in[:, :hidden_width] + weight_partner(
        dn_in[:, hidden_width:].astype(bf16)
    ).astype(f32)
    mixed = (y_own + RESIDUAL * own_rows(moe_pair)).astype(bf16)

    grad_heads = dot_f32(grad_attn, w_out, 1, 1).astype(bf16)
    grad_out_w = contract_rows(heads_out, grad_attn).astype(bf16)
    dq_raw, dk_raw, dv_raw = pl.pallas_call(
        attention_backward,
        out_shape=(
            jax.ShapeDtypeStruct((length, q_width), bf16),
            jax.ShapeDtypeStruct((length, k_width), bf16),
            jax.ShapeDtypeStruct((length, k_width), bf16),
        ),
        in_specs=[whole_spec()] * 8,
        out_specs=(whole_spec(),) * 3,
        scratch_shapes=[
            pltpu.VMEM((length, q_width), f32),
            pltpu.VMEM((length, k_width), f32),
            pltpu.VMEM((length, k_width), f32),
        ],
        compiler_params=params,
        cost_estimate=pl.CostEstimate(
            flops=12 * length * length * q_width, bytes_accessed=8 * length * q_width, transcendentals=length * length * 4
        ),
        name="attention_backward",
    )(queries, keys, values, grad_heads, cos_t, sin_t, seg_col, seg_row)
    summed = dot_f32(dq_raw, w_query, 1, 1) + dot_f32(dk_raw, w_key, 1, 1)
    summed = summed + dot_f32(dv_raw, w_value, 1, 1)
    summed_b = summed.astype(bf16)
    dh1 = lax.dynamic_slice_in_dim(summed, mine * rows_dev, rows_dev, 0)
    for step in range(1, tensors):
        start = ((mine + step) % tensors) * rows_dev
        sent = lax.dynamic_slice_in_dim(summed_b, start, rows_dev, 0)
        dh1 = dh1 + shifted(sent, step).astype(f32)
    grad_norm1 = lax.psum(jnp.sum(summed * (x_all * r1), axis=0), ("expert", "tensor"))
    grad_q, grad_k, grad_v, grad_out_w = lax.psum(
        (
            contract_rows(h1, dq_raw).astype(bf16),
            contract_rows(h1, dk_raw).astype(bf16),
            contract_rows(h1, dv_raw).astype(bf16),
            grad_out_w,
        ),
        "expert",
    )
    x_own = tokens.astype(f32)
    r1_own = lax.rsqrt(jnp.mean(x_own * x_own, axis=-1, keepdims=True) + EPSILON)
    n1 = x_own * r1_own
    dn1 = dh1 * norm1_gain
    grad_input = dy + r1_own * (dn1 - n1 * jnp.mean(dn1 * n1, axis=-1, keepdims=True))
    return (
        mixed,
        grad_input,
        grad_norm1,
        grad_q.astype(f32),
        grad_k.astype(f32),
        grad_v.astype(f32),
        grad_out_w.astype(f32),
        grad_norm2,
        grad_rt.T,
        grad_gate,
        grad_up,
        grad_down,
    )


def choose_plan(mesh):
    def per_device(tokens, *rest):
        gathered = tokens.size * 2 * mesh.shape["expert"] * mesh.shape["tensor"]
        fits = gathered <= GATHER_LIMIT and mesh.shape["tensor"] == 4
        plan = per_device_tokens if fits else per_device_slots
        return plan(tokens, *rest)

    return per_device


def solution(mesh):
    return jax.shard_map(
        choose_plan(mesh),
        mesh=mesh,
        in_specs=(
            P(("expert", "tensor"), None),
            P("expert"),
            P(("expert", "tensor"), None),
            P(("expert", "tensor"), None),
            P(),
            P(None, "tensor"),
            P(None, "tensor"),
            P(None, "tensor"),
            P("tensor", None),
            P(),
            P(),
            P("expert", None, "tensor"),
            P("expert", None, "tensor"),
            P("expert", "tensor", None),
            P(("expert", "tensor"), None),
        ),
        out_specs=(
            P(("expert", "tensor"), None),
            P(("expert", "tensor"), None),
            P(),
            P(None, "tensor"),
            P(None, "tensor"),
            P(None, "tensor"),
            P("tensor", None),
            P(),
            P(),
            P("expert", None, "tensor"),
            P("expert", None, "tensor"),
            P("expert", "tensor", None),
        ),
        check_vma=False,
    )
```
